32 devices in a mesh: str: 16 (over z, y, x), chol: 2 (over core).
Axes of the slice: x: 2, y: 2, z: 4, core: 2. Of those that a mesh axis runs over, the one named last changes fastest.
Arguments:
- amplitudes: bfloat16 [4, 2048, 2048], P(None, 'str'), may hold values from -6 to 6
- alpha_values: bfloat16 [2, 16, 8, 128, 128], P('chol'), may hold values from -0.1875 to 0.1875
- alpha_cols: int32 [2, 16, 8], P('chol'), may hold values from 0 to 15, all different within a row
- beta_values: bfloat16 [2, 16, 8, 128, 128], P('chol'), may hold values from -0.1875 to 0.1875
- beta_cols: int32 [2, 16, 8], P('chol'), may hold values from 0 to 15, all different within a row
Outputs:
- sigma: float32 [4, 2048, 2048], P(None, 'chol', 'str')
The draws below stay inside these ranges and needn't reach their ends.
Inputs may be any that keep to these rules, and one draw needn't show every extreme that they name: `alpha_cols`: within one block row the 8 block columns are distinct. `beta_cols`: within one block row the 8 block columns are distinct.
All inputs are finite; a program needn't handle non-finite values.
Results may differ from the reference program's by a relative error of at most 0.0029.
Values may be sent and summed in bfloat16 or wider, within the bound.
A program may use at most 128 MiB of HBM per device.

```python
import jax
import jax.numpy as jnp
from jax import lax

BLK = 128
NNZ = 8
R = 4
NA = 2048
NB = 2048
NBLK = 16
K = 2


def block_scale(rng, shape, pieces, smallest, high):
    gain = 1.0
    for axis_at, blocks in pieces:
        heights = jax.random.uniform(jax.random.fold_in(jax.random.fold_in(rng, 6), axis_at), (blocks,), jnp.float32, smallest / len(pieces), high / len(pieces))
        gain = gain * jnp.repeat(jnp.exp(heights), shape[axis_at] // blocks).reshape((-1,) + (1,) * (len(shape) - 1 - axis_at))
    return gain


def choose_distinct(key, rows, number_of, top, lift):
    order = jax.random.permutation(jax.random.fold_in(key, 1), number_of)
    pull = order
    for power in range(3):
        pull = pull * pull // number_of
    pull = pull * lift // number_of
    tickets = jax.random.randint(jax.random.fold_in(key, 2), (rows, number_of), 0, 4096) + pull
    fixed_rows = jax.random.permutation(jax.random.fold_in(key, 3), rows)[jnp.arange(number_of) % rows]
    tickets = jnp.where(jnp.arange(rows)[:, None] == fixed_rows[None, :], 1 << 14, tickets)
    score = tickets * number_of + jnp.arange(number_of)
    return lax.top_k(score.astype(jnp.int32), top)[1].astype(jnp.int32)


def gaussian(key, shape, scale, bound, split=(), held_as=jnp.bfloat16):
    factor_of = block_scale(key, shape, split, -0.22, 0.18) if split else 1.0
    drawn = jax.random.normal(key, shape, jnp.float32) * scale * factor_of
    return jnp.minimum(jnp.maximum(drawn, -bound), bound).astype(held_as)


def setup_inputs(seed: int = 0) -> dict:
    seeds = jax.random.split(jax.random.key(seed), 6)
    amplitudes = gaussian(seeds[0], (R, NA, NB), 1.0, 6.0, ((1, 16),))
    alpha_values = gaussian(seeds[1], (K, NBLK, NNZ, BLK, BLK), (NNZ * BLK) ** -0.5, 0.1875, ((0, 2),))
    alpha_cols = choose_distinct(seeds[2], K * NBLK, NBLK, NNZ, 0).reshape((K, NBLK, NNZ))
    beta_values = gaussian(seeds[3], (K, NBLK, NNZ, BLK, BLK), (NNZ * BLK) ** -0.5, 0.1875, ((0, 2),))
    beta_cols = choose_distinct(seeds[4], K * NBLK, NBLK, NNZ, 0).reshape((K, NBLK, NNZ))
    return {"amplitudes": amplitudes, "alpha_values": alpha_values, "alpha_cols": alpha_cols, "beta_values": beta_values, "beta_cols": beta_cols}


def beta_side(amplitudes, values, cols):
    nvec, na, nb = amplitudes.shape
    blk = values.shape[-1]
    nblk = nb // blk
    blocks = amplitudes.reshape(nvec, na, nblk, blk)

    def one_row(j):
        picked = jnp.take(blocks, cols[j], axis=2).astype(jnp.float32)
        return jnp.einsum('ramc,mdc->rad', picked, values[j].astype(jnp.float32))

    parts = lax.map(one_row, jnp.arange(nblk, dtype=jnp.int32))
    return jnp.transpose(parts, (1, 2, 0, 3)).reshape(nvec, na, nb).astype(jnp.bfloat16)


def alpha_side(half, values, cols):
    nvec, na, nb = half.shape
    blk = values.shape[-1]
    nblk = na // blk
    blocks = half.reshape(nvec, nblk, blk, nb)

    def one_row(i):
        picked = jnp.take(blocks, cols[i], axis=1).astype(jnp.float32)
        return jnp.einsum('rmcq,mdc->rdq', picked, values[i].astype(jnp.float32))

    parts = lax.map(one_row, jnp.arange(nblk, dtype=jnp.int32))
    return jnp.transpose(parts, (1, 0, 2, 3)).reshape(nvec, na, nb)


def reference(amplitudes, alpha_values, alpha_cols, beta_values, beta_cols):
    total = jnp.zeros(amplitudes.shape, jnp.float32)
    for vector in range(K):
        half = beta_side(amplitudes, beta_values[vector], beta_cols[vector])
        total = total + alpha_side(half, alpha_values[vector], alpha_cols[vector])
    return total
```

```python
import functools

import jax
import jax.numpy as jnp
from jax import lax
from jax.experimental import pallas as pl
from jax.experimental.pallas import tpu as pltpu
from jax.sharding import PartitionSpec as P

MESH = pl.DeviceIdType.MESH


def partner(me, step, count):
    if count % 2:
        return (me + 1 + step) % count
    half = count // 2
    side, place = me // half, me % half
    across = (step + 1) % 2
    other = side + across - 2 * side * across
    return other * half + (place + (step + 1) // 2) % half


def kernel(
    n, nchol, nvec, nblk, nnz, blk,
    acols, bcols, amp_hbm, aval_hbm, bval_hbm, out,
    amp, aval, bval, send, tsend, trecv, *rest,
):
    recv = rest[:nvec]
    amp_sem, aval_sem, bval_sem, send_sem, recv_sem, tsend_sem, trecv_sem = rest[nvec:]
    me, core = lax.axis_index("str"), lax.axis_index("chol")
    share = nblk // nchol

    def load_amp(c):
        return pltpu.make_async_copy(
            amp_hbm.at[:, :, pl.ds(pl.multiple_of(c * blk, blk), blk)], amp.at[c], amp_sem.at[c]
        )

    def start_amp(c, carry):
        load_amp(c).start()
        return carry

    def wait_amp(c, carry):
        load_amp(c).wait()
        return carry

    lax.fori_loop(0, nblk, start_amp, 0)

    def load_beta(step, j):
        return pltpu.make_async_copy(bval_hbm.at[j], bval.at[j], bval_sem.at[step])

    def start_beta(step, carry):
        load_beta(step, partner(me, step, n)).start()
        return carry

    lax.fori_loop(0, n - 1, start_beta, 0)
    load_beta(n - 1, me).start()
    load_alpha = pltpu.make_async_copy(aval_hbm, aval, aval_sem)
    load_alpha.start()

    barrier = pltpu.get_barrier_semaphore()

    def greet(step, carry):
        pl.semaphore_signal(
            barrier, inc=1, device_id={"str": (me + 1 + step) % n, "chol": core}, device_id_type=MESH
        )
        return carry

    lax.fori_loop(0, n - 1, greet, 0)
    for o in range(1, nchol):
        pl.semaphore_signal(
            barrier, inc=1, device_id={"str": me, "chol": (core + o) % nchol}, device_id_type=MESH
        )
    lax.fori_loop(0, nblk, wait_amp, 0)
    pl.semaphore_wait(barrier, n - 1 + nchol - 1)

    def beta_block(step, j):
        load_beta(step, j).wait()
        total = None
        for m in range(0, nnz, 2):
            left, right = [], []
            for b in range(m, min(m + 2, nnz)):
                left.append(amp[bcols[j, b]].reshape(nvec * blk, blk))
                right.append(bval[j, b])
            part = lax.dot_general(
                jnp.concatenate(left, axis=1), jnp.concatenate(right, axis=1),
                (((1,), (1,)), ((), ())), preferred_element_type=jnp.float32,
            )
            total = part if total is None else total + part
        return total.astype(jnp.bfloat16).reshape(nvec, blk, blk)

    def give(r, step):
        return pltpu.make_async_remote_copy(
            src_ref=send.at[r, step],
            dst_ref=recv[r].at[me],
            send_sem=send_sem.at[r],
            recv_sem=recv_sem.at[r],
            device_id={"str": partner(me, step, n), "chol": core},
            device_id_type=MESH,
        )

    def beta_step(step, carry):
        half = beta_block(step, partner(me, step, n))
        for r in range(nvec):
            send[r, step] = half[r]
        give(0, step).start()
        return carry

    lax.fori_loop(0, n - 1, beta_step, 0)
    for r in range(1, nvec):
        def start_give(step, carry, r=r):
            give(r, step).start()
            return carry

        lax.fori_loop(0, n - 1, start_give, 0)

    mine = beta_block(n - 1, me)
    for r in range(nvec):
        recv[r][me] = mine[r]
    load_alpha.wait()

    def alpha_block(r, i):
        left = jnp.concatenate([aval[i, m] for m in range(nnz)], axis=1)
        right = jnp.concatenate([recv[r][acols[i, m]] for m in range(nnz)], axis=0)
        return jnp.dot(left, right, preferred_element_type=jnp.float32)

    def exchange(o, r):
        return pltpu.make_async_remote_copy(
            src_ref=tsend.at[o - 1, r],
            dst_ref=trecv.at[o - 1, r],
            send_sem=tsend_sem.at[o - 1, r],
            recv_sem=trecv_sem.at[o - 1, r],
            device_id={"str": me, "chol": (core + o) % nchol},
            device_id_type=MESH,
        )

    def finish(r):
        for o in range(1, nchol):
            exchange(o, r).wait_recv()
            out[r] += trecv[o - 1, r]

    for r in range(nvec):
        if n > 1:
            landed = recv[r].at[pl.ds(0, n - 1)]
            pltpu.make_async_copy(landed, landed, recv_sem.at[r]).wait()
        for o in range(1, nchol):
            first = ((core + o) % nchol) * share

            def theirs(b, carry, o=o, r=r, first=first):
                tsend[o - 1, r, pl.ds(pl.multiple_of(b * blk, blk), blk), :] = alpha_block(r, first + b)
                return carry

            lax.fori_loop(0, share, theirs, 0)
            exchange(o, r).start()

        def ours(b, carry, r=r):
            out[r, pl.ds(pl.multiple_of(b * blk, blk), blk), :] = alpha_block(r, core * share + b)
            return carry

        lax.fori_loop(0, share, ours, 0)
        if r:
            finish(r - 1)
    finish(nvec - 1)

    for r in range(nvec):
        if n > 1:
            sent = send.at[r, pl.ds(0, n - 1)]
            pltpu.make_async_copy(sent, sent, send_sem.at[r]).wait()
        for o in range(1, nchol):
            exchange(o, r).wait_send()


def body(n, nchol, amplitudes, alpha_values, alpha_cols, beta_values, beta_cols):
    nvec, rows, width = amplitudes.shape
    _, nblk, nnz, blk, _ = beta_values.shape
    assert rows == blk and width == n * blk and nblk == n
    out_rows = nblk * blk // nchol
    dma = pltpu.SemaphoreType.DMA
    others = max(nchol - 1, 1)
    half = (n, blk, blk)
    smem = pl.BlockSpec(memory_space=pltpu.SMEM)
    anywhere = pl.BlockSpec(memory_space=pl.ANY)
    return pl.pallas_call(
        functools.partial(kernel, n, nchol, nvec, nblk, nnz, blk),
        out_shape=jax.ShapeDtypeStruct((nvec, out_rows, blk), jnp.float32),
        in_specs=[smem, smem, anywhere, anywhere, anywhere],
        out_specs=pl.BlockSpec(memory_space=pltpu.VMEM),
        scratch_shapes=[
            pltpu.VMEM((nblk, nvec, blk, blk), jnp.bfloat16),
            pltpu.VMEM(alpha_values.shape[1:], jnp.bfloat16),
            pltpu.VMEM(beta_values.shape[1:], jnp.bfloat16),
            pltpu.VMEM((nvec,) + half, jnp.bfloat16),
            pltpu.VMEM((others, nvec, out_rows, blk), jnp.float32),
            pltpu.VMEM((others, nvec, out_rows, blk), jnp.float32),
            *[pltpu.VMEM(half, jnp.bfloat16) for _ in range(nvec)],
            dma((nblk,)), dma, dma((n,)), dma((nvec,)), dma((nvec,)),
            dma((others, nvec)), dma((others, nvec)),
        ],
        compiler_params=pltpu.CompilerParams(
            collective_id=0, has_side_effects=True, vmem_limit_bytes=48 * 1024 * 1024
        ),
        cost_estimate=pl.CostEstimate(
            flops=8 * nvec * nblk * nnz * blk**3, bytes_accessed=2**24, transcendentals=0
        ),
    )(alpha_cols[0], beta_cols[0], amplitudes, alpha_values[0], beta_values[0])


def solution(mesh):
    placed = (
        P(None, "str", None),
        P("chol", None, None, None, None),
        P("chol", None, None),
        P("chol", None, None, None, None),
        P("chol", None, None),
    )
    return jax.shard_map(
        functools.partial(body, mesh.shape["str"], mesh.shape["chol"]),
        mesh=mesh, in_specs=placed, out_specs=P(None, "chol", "str"), check_vma=False,
    )
```

```python
import functools

import jax
import jax.numpy as jnp
from jax import lax
from jax.experimental import pallas as pl
from jax.experimental.pallas import tpu as pltpu
from jax.sharding import PartitionSpec as P

MESH = pl.DeviceIdType.MESH


def partner(me, step, count):
    if count % 2:
        return (me + 1 + step) % count
    half = count // 2
    side, place = me // half, me % half
    here = step // half
    other = (side + 1 + here) % 2
    return other * half + (place + step + here) % half


def kernel(
    n, nchol, nvec, nblk, nnz, blk,
    acols, bcols, amp_hbm, aval_hbm, bval_hbm, out_hbm,
    amp, aval, bval, send, tsend, trecv, out, *rest,
):
    recv = rest[:nvec]
    amp_sem, aval_sem, bval_sem, send_sem, recv_sem, tsend_sem, trecv_sem, out_sem = rest[nvec:]
    me, core = lax.axis_index("str"), lax.axis_index("chol")
    share = nblk // nchol

    barrier = pltpu.get_barrier_semaphore()

    def greet(step, carry):
        pl.semaphore_signal(
            barrier, inc=1, device_id={"str": (me + 1 + step) % n, "chol": core}, device_id_type=MESH
        )
        return carry

    lax.fori_loop(0, n - 1, greet, 0)
    for o in range(1, nchol):
        pl.semaphore_signal(
            barrier, inc=1, device_id={"str": me, "chol": (core + o) % nchol}, device_id_type=MESH
        )
    def load_amp(c):
        return pltpu.make_async_copy(
            amp_hbm.at[:, :, pl.ds(pl.multiple_of(c * blk, blk), blk)], amp.at[c], amp_sem.at[c]
        )

    def start_amp(c, carry):
        load_amp(c).start()
        return carry

    def wait_amp(c, carry):
        load_amp(c).wait()
        return carry

    lax.fori_loop(0, nblk, start_amp, 0)

    def load_beta(step, j):
        return pltpu.make_async_copy(bval_hbm.at[j], bval.at[j], bval_sem.at[step])

    def start_beta(step, carry):
        load_beta(step, partner(me, step, n)).start()
        return carry

    lax.fori_loop(0, n - 1, start_beta, 0)
    load_beta(n - 1, me).start()
    load_alpha = pltpu.make_async_copy(aval_hbm, aval, aval_sem)
    load_alpha.start()

    lax.fori_loop(0, nblk, wait_amp, 0)
    def beta_block(step, j):
        load_beta(step, j).wait()
        total = None
        for m in range(0, nnz, 2):
            left, right = [], []
            for b in range(m, min(m + 2, nnz)):
                left.append(amp[bcols[b, j]].reshape(nvec * blk, blk))
                right.append(bval[j, b])
            part = lax.dot_general(
                jnp.concatenate(left, axis=1), jnp.concatenate(right, axis=1),
                (((1,), (1,)), ((), ())), preferred_element_type=jnp.float32,
            )
            total = part if total is None else total + part
        return total.astype(jnp.bfloat16).reshape(nvec, blk, blk)

    def give(r, step):
        return pltpu.make_async_remote_copy(
            src_ref=send.at[r, step],
            dst_ref=recv[r].at[me],
            send_sem=send_sem.at[r],
            recv_sem=recv_sem.at[r],
            device_id={"str": partner(me, step, n), "chol": core},
            device_id_type=MESH,
        )

    def beta_step(step, carry):
        half = beta_block(step, partner(me, step, n))
        for r in range(nvec):
            send[r, step] = half[r]
        return carry

    def beta_send(step, carry):
        beta_step(step, carry)
        give(0, step).start()
        return carry

    lead = min(1, n - 1)
    lax.fori_loop(0, lead, beta_step, 0)
    pl.semaphore_wait(barrier, n - 1 + nchol - 1)
    for step in range(lead):
        give(0, step).start()
    lax.fori_loop(lead, n - 1, beta_send, 0)
    for r in range(1, nvec):
        def start_give(step, carry, r=r):
            give(r, step).start()
            return carry

        lax.fori_loop(0, n - 1, start_give, 0)

    mine = beta_block(n - 1, me)
    for r in range(nvec):
        recv[r][me] = mine[r]
    load_alpha.wait()

    def alpha_block(r, i):
        left = jnp.concatenate([aval[i, m] for m in range(nnz)], axis=1)
        right = jnp.concatenate([recv[r][acols[m, i]] for m in range(nnz)], axis=0)
        return jnp.dot(left, right, preferred_element_type=jnp.float32)

    def exchange(o, r):
        return pltpu.make_async_remote_copy(
            src_ref=tsend.at[o - 1, r],
            dst_ref=trecv.at[o - 1, r],
            send_sem=tsend_sem.at[o - 1, r],
            recv_sem=trecv_sem.at[o - 1, r],
            device_id={"str": me, "chol": (core + o) % nchol},
            device_id_type=MESH,
        )

    def store(r):
        return pltpu.make_async_copy(out.at[r], out_hbm.at[r], out_sem.at[r])

    def finish(r):
        for o in range(1, nchol):
            exchange(o, r).wait_recv()
            out[r] += trecv[o - 1, r]
        store(r).start()

    for r in range(nvec):
        if n > 1:
            landed = recv[r].at[pl.ds(0, n - 1)]
            pltpu.make_async_copy(landed, landed, recv_sem.at[r]).wait()
        for o in range(1, nchol):
            first = ((core + o) % nchol) * share

            def theirs(b, carry, o=o, r=r, first=first):
                tsend[o - 1, r, pl.ds(pl.multiple_of(b * blk, blk), blk), :] = alpha_block(r, first + b)
                return carry

            lax.fori_loop(0, share, theirs, 0)
            exchange(o, r).start()

        def ours(b, carry, r=r):
            out[r, pl.ds(pl.multiple_of(b * blk, blk), blk), :] = alpha_block(r, core * share + b)
            return carry

        lax.fori_loop(0, share, ours, 0)
        if r:
            finish(r - 1)
    finish(nvec - 1)

    for r in range(nvec):
        if n > 1:
            sent = send.at[r, pl.ds(0, n - 1)]
            pltpu.make_async_copy(sent, sent, send_sem.at[r]).wait()
        for o in range(1, nchol):
            exchange(o, r).wait_send()
        store(r).wait()


def body(n, nchol, amplitudes, alpha_values, alpha_cols, beta_values, beta_cols):
    nvec, rows, width = amplitudes.shape
    _, nblk, nnz, blk, _ = beta_values.shape
    assert rows == blk and width == n * blk and nblk == n
    out_rows = nblk * blk // nchol
    dma = pltpu.SemaphoreType.DMA
    others = max(nchol - 1, 1)
    half = (n, blk, blk)
    smem = pl.BlockSpec(memory_space=pltpu.SMEM)
    hbm = pl.BlockSpec(memory_space=pltpu.HBM)
    return pl.pallas_call(
        functools.partial(kernel, n, nchol, nvec, nblk, nnz, blk),
        out_shape=jax.ShapeDtypeStruct((nvec, out_rows, blk), jnp.float32),
        in_specs=[smem, smem, hbm, hbm, hbm],
        out_specs=hbm,
        scratch_shapes=[
            pltpu.VMEM((nblk, nvec, blk, blk), jnp.bfloat16),
            pltpu.VMEM(alpha_values.shape[1:], jnp.bfloat16),
            pltpu.VMEM(beta_values.shape[1:], jnp.bfloat16),
            pltpu.VMEM((nvec,) + half, jnp.bfloat16),
            pltpu.VMEM((others, nvec, out_rows, blk), jnp.float32),
            pltpu.VMEM((others, nvec, out_rows, blk), jnp.float32),
            pltpu.VMEM((nvec, out_rows, blk), jnp.float32),
            *[pltpu.VMEM(half, jnp.bfloat16) for _ in range(nvec)],
            dma((nblk,)), dma, dma((n,)), dma((nvec,)), dma((nvec,)),
            dma((others, nvec)), dma((others, nvec)), dma((nvec,)),
        ],
        compiler_params=pltpu.CompilerParams(
            collective_id=0, has_side_effects=True, vmem_limit_bytes=56 * 1024 * 1024
        ),
        cost_estimate=pl.CostEstimate(
            flops=8 * nvec * nblk * nnz * blk**3, bytes_accessed=2**24, transcendentals=0
        ),
    )(alpha_cols[0].T, beta_cols[0].T, amplitudes, alpha_values[0], beta_values[0])


def solution(mesh):
    placed = (
        P(None, "str", None),
        P("chol", None, None, None, None),
        P("chol", None, None),
        P("chol", None, None, None, None),
        P("chol", None, None),
    )
    return jax.shard_map(
        functools.partial(body, mesh.shape["str"], mesh.shape["chol"]),
        mesh=mesh, in_specs=placed, out_specs=P(None, "chol", "str"), check_vma=False,
    )
```

```python
import functools

import jax
import jax.numpy as jnp
from jax import lax
from jax.experimental import pallas as pl
from jax.experimental.pallas import tpu as pltpu
from jax.sharding import PartitionSpec as P

MESH = pl.DeviceIdType.MESH


def partner(me, step, count):
    if count % 2:
        return (me + 1 + step) % count
    half = count // 2
    side, place = me // half, me % half
    here = step // half
    other = (side + 1 + here) % 2
    return other * half + (place + step + here) % half


def kernel(
    n, nchol, nvec, nblk, nnz, blk,
    acols, bcols, amp_hbm, aval_hbm, bval_hbm, out_hbm,
    amp, aval, bval, send, tsend, trecv, out, *rest,
):
    recv = rest[:nvec]
    amp_sem, aval_sem, bval_sem, send_sem, recv_sem, tsend_sem, trecv_sem, out_sem = rest[nvec:]
    me, core = lax.axis_index("str"), lax.axis_index("chol")
    share = nblk // nchol

    barrier = pltpu.get_barrier_semaphore()

    def greet(step, carry):
        pl.semaphore_signal(
            barrier, inc=1, device_id={"str": (me + 1 + step) % n, "chol": core}, device_id_type=MESH
        )
        return carry

    lax.fori_loop(0, n - 1, greet, 0)
    for o in range(1, nchol):
        pl.semaphore_signal(
            barrier, inc=1, device_id={"str": me, "chol": (core + o) % nchol}, device_id_type=MESH
        )
    def load_amp(c):
        return pltpu.make_async_copy(
            amp_hbm.at[:, :, pl.ds(pl.multiple_of(c * blk, blk), blk)], amp.at[c], amp_sem.at[c]
        )

    def start_amp(c, carry):
        load_amp(c).start()
        return carry

    def wait_amp(c, carry):
        load_amp(c).wait()
        return carry

    lax.fori_loop(0, nblk, start_amp, 0)

    def load_beta(step, j):
        return pltpu.make_async_copy(bval_hbm.at[j], bval.at[j], bval_sem.at[step])

    def start_beta(step, carry):
        load_beta(step, partner(me, step, n)).start()
        return carry

    lax.fori_loop(0, n - 1, start_beta, 0)
    load_beta(n - 1, me).start()
    load_alpha = pltpu.make_async_copy(aval_hbm, aval, aval_sem)

    lax.fori_loop(0, nblk, wait_amp, 0)
    def beta_block(step, j):
        load_beta(step, j).wait()
        total = None
        for m in range(0, nnz, 2):
            left, right = [], []
            for b in range(m, min(m + 2, nnz)):
                left.append(amp[bcols[b, j]].reshape(nvec * blk, blk))
                right.append(bval[j, b])
            part = lax.dot_general(
                jnp.concatenate(left, axis=1), jnp.concatenate(right, axis=1),
                (((1,), (1,)), ((), ())), preferred_element_type=jnp.float32,
            )
            total = part if total is None else total + part
        return total.astype(jnp.bfloat16).reshape(nvec, blk, blk)

    def give(r, step):
        return pltpu.make_async_remote_copy(
            src_ref=send.at[r, step],
            dst_ref=recv[r].at[me],
            send_sem=send_sem.at[r],
            recv_sem=recv_sem.at[r],
            device_id={"str": partner(me, step, n), "chol": core},
            device_id_type=MESH,
        )

    def beta_step(step, carry):
        half = beta_block(step, partner(me, step, n))
        for r in range(nvec):
            send[r, step] = half[r]
        return carry

    def beta_send(step, carry):
        beta_step(step, carry)
        give(0, step).start()
        return carry

    lead = min(1, n - 1)
    lax.fori_loop(0, lead, beta_step, 0)
    pl.semaphore_wait(barrier, n - 1 + nchol - 1)
    for step in range(lead):
        give(0, step).start()
    lax.fori_loop(lead, n - 1, beta_send, 0)
    for r in range(1, nvec):
        def start_give(step, carry, r=r):
            give(r, step).start()
            return carry

        def start_both(step, carry, r=r):
            give(r, far + step - 1).start()
            give(r, step).start()
            return carry

        far = n // 2 if n % 2 == 0 else n - 1
        lax.fori_loop(0, 1 if far < n - 1 else far, start_give, 0)
        if far < n - 1:
            lax.fori_loop(1, far, start_both, 0)
    load_alpha.start()

    mine = beta_block(n - 1, me)
    for r in range(nvec):
        recv[r][me] = mine[r]
    load_alpha.wait()

    def alpha_block(r, i):
        left = jnp.concatenate([aval[i, m] for m in range(nnz)], axis=1)
        right = jnp.concatenate([recv[r][acols[m, i]] for m in range(nnz)], axis=0)
        return jnp.dot(left, right, preferred_element_type=jnp.float32)

    def exchange(o, r):
        return pltpu.make_async_remote_copy(
            src_ref=tsend.at[o - 1, r],
            dst_ref=trecv.at[o - 1, r],
            send_sem=tsend_sem.at[o - 1, r],
            recv_sem=trecv_sem.at[o - 1, r],
            device_id={"str": me, "chol": (core + o) % nchol},
            device_id_type=MESH,
        )

    def store(r):
        return pltpu.make_async_copy(out.at[r], out_hbm.at[r], out_sem.at[r])

    def finish(r):
        for o in range(1, nchol):
            exchange(o, r).wait_recv()
            out[r] += trecv[o - 1, r]
        store(r).start()

    for r in range(nvec):
        if n > 1:
            landed = recv[r].at[pl.ds(0, n - 1)]
            pltpu.make_async_copy(landed, landed, recv_sem.at[r]).wait()
        for o in range(1, nchol):
            first = ((core + o) % nchol) * share

            def theirs(b, carry, o=o, r=r, first=first):
                tsend[o - 1, r, pl.ds(pl.multiple_of(b * blk, blk), blk), :] = alpha_block(r, first + b)
                return carry

            lax.fori_loop(0, share, theirs, 0)
            exchange(o, r).start()

        def ours(b, carry, r=r):
            out[r, pl.ds(pl.multiple_of(b * blk, blk), blk), :] = alpha_block(r, core * share + b)
            return carry

        lax.fori_loop(0, share, ours, 0)
        if r:
            finish(r - 1)
    finish(nvec - 1)

    for r in range(nvec):
        if n > 1:
            sent = send.at[r, pl.ds(0, n - 1)]
            pltpu.make_async_copy(sent, sent, send_sem.at[r]).wait()
        for o in range(1, nchol):
            exchange(o, r).wait_send()
        store(r).wait()


def body(n, nchol, amplitudes, alpha_values, alpha_cols, beta_values, beta_cols):
    nvec, rows, width = amplitudes.shape
    _, nblk, nnz, blk, _ = beta_values.shape
    assert rows == blk and width == n * blk and nblk == n
    out_rows = nblk * blk // nchol
    dma = pltpu.SemaphoreType.DMA
    others = max(nchol - 1, 1)
    half = (n, blk, blk)
    smem = pl.BlockSpec(memory_space=pltpu.SMEM)
    hbm = pl.BlockSpec(memory_space=pltpu.HBM)
    return pl.pallas_call(
        functools.partial(kernel, n, nchol, nvec, nblk, nnz, blk),
        out_shape=jax.ShapeDtypeStruct((nvec, out_rows, blk), jnp.float32),
        in_specs=[smem, smem, hbm, hbm, hbm],
        out_specs=hbm,
        scratch_shapes=[
            pltpu.VMEM((nblk, nvec, blk, blk), jnp.bfloat16),
            pltpu.VMEM(alpha_values.shape[1:], jnp.bfloat16),
            pltpu.VMEM(beta_values.shape[1:], jnp.bfloat16),
            pltpu.VMEM((nvec,) + half, jnp.bfloat16),
            pltpu.VMEM((others, nvec, out_rows, blk), jnp.float32),
            pltpu.VMEM((others, nvec, out_rows, blk), jnp.float32),
            pltpu.VMEM((nvec, out_rows, blk), jnp.float32),
            *[pltpu.VMEM(half, jnp.bfloat16) for _ in range(nvec)],
            dma((nblk,)), dma, dma((n,)), dma((nvec,)), dma((nvec,)),
            dma((others, nvec)), dma((others, nvec)), dma((nvec,)),
        ],
        compiler_params=pltpu.CompilerParams(
            collective_id=0, has_side_effects=True, vmem_limit_bytes=51 * 1024 * 1024
        ),
        cost_estimate=pl.CostEstimate(
            flops=8 * nvec * nblk * nnz * blk**3, bytes_accessed=2**24, transcendentals=0
        ),
    )(alpha_cols[0].T, beta_cols[0].T, amplitudes, alpha_values[0], beta_values[0])


def solution(mesh):
    placed = (
        P(None, "str", None),
        P("chol", None, None, None, None),
        P("chol", None, None),
        P("chol", None, None, None, None),
        P("chol", None, None),
    )
    return jax.shard_map(
        functools.partial(body, mesh.shape["str"], mesh.shape["chol"]),
        mesh=mesh, in_specs=placed, out_specs=P(None, "chol", "str"), check_vma=False,
    )
```

```python
import functools

import jax
import jax.numpy as jnp
from jax import lax
from jax.experimental import pallas as pl
from jax.experimental.pallas import tpu as pltpu
from jax.sharding import PartitionSpec as P

MESH = pl.DeviceIdType.MESH


def partner(me, step, count):
    if count % 2:
        return (me + 1 + step) % count
    half = count // 2
    side, place = me // half, me % half
    here = step // half
    other = (side + 1 + here) % 2
    return other * half + (place + step + here) % half


def kernel(
    n, nchol, nvec, nblk, nnz, blk,
    acols, bcols, amp_hbm, aval_hbm, bval_hbm, out_hbm,
    amp, aval, bval, send, tsend, trecv, out, *rest,
):
    recv = rest[:nvec]
    amp_sem, aval_sem, bval_sem, send_sem, recv_sem, tsend_sem, trecv_sem, out_sem = rest[nvec:]
    me, core = lax.axis_index("str"), lax.axis_index("chol")
    share = nblk // nchol

    barrier = pltpu.get_barrier_semaphore()

    def greet(step, carry):
        pl.semaphore_signal(
            barrier, inc=1, device_id={"str": (me + 1 + step) % n, "chol": core}, device_id_type=MESH
        )
        return carry

    lax.fori_loop(0, n - 1, greet, 0)
    for o in range(1, nchol):
        pl.semaphore_signal(
            barrier, inc=1, device_id={"str": me, "chol": (core + o) % nchol}, device_id_type=MESH
        )
    def load_amp(c):
        return pltpu.make_async_copy(
            amp_hbm.at[:, :, pl.ds(pl.multiple_of(c * blk, blk), blk)], amp.at[c], amp_sem.at[c]
        )

    def start_amp(c, carry):
        load_amp(c).start()
        return carry

    def wait_amp(c, carry):
        load_amp(c).wait()
        return carry

    lax.fori_loop(0, nblk, start_amp, 0)

    def load_beta(step, j):
        return pltpu.make_async_copy(bval_hbm.at[j], bval.at[j], bval_sem.at[step])

    def start_beta(step, carry):
        load_beta(step, partner(me, step, n)).start()
        return carry

    lax.fori_loop(0, n - 1, start_beta, 0)
    load_beta(n - 1, me).start()
    load_alpha = pltpu.make_async_copy(aval_hbm, aval, aval_sem)

    lax.fori_loop(0, nblk, wait_amp, 0)
    def beta_block(step, j):
        load_beta(step, j).wait()
        total = None
        for m in range(0, nnz, 2):
            left, right = [], []
            for b in range(m, min(m + 2, nnz)):
                left.append(amp[bcols[b, j]].reshape(nvec * blk, blk))
                right.append(bval[j, b])
            part = lax.dot_general(
                jnp.concatenate(left, axis=1), jnp.concatenate(right, axis=1),
                (((1,), (1,)), ((), ())), preferred_element_type=jnp.float32,
            )
            total = part if total is None else total + part
        return total.astype(jnp.bfloat16).reshape(nvec, blk, blk)

    def give(r, step):
        return pltpu.make_async_remote_copy(
            src_ref=send.at[r, step],
            dst_ref=recv[r].at[me],
            send_sem=send_sem.at[r],
            recv_sem=recv_sem.at[r],
            device_id={"str": partner(me, step, n), "chol": core},
            device_id_type=MESH,
        )

    def beta_step(step, carry):
        half = beta_block(step, partner(me, step, n))
        for r in range(nvec):
            send[r, step] = half[r]
        return carry

    def beta_send(step, carry):
        beta_step(step, carry)
        give(0, step).start()
        return carry

    def beta_both(step, carry):
        beta_step(step, carry)
        give(0, step).start()
        if nvec > 1:
            give(1, step - far).start()
        if nvec == 2:
            give(1, step).start()
        return carry

    far = n // 2 if n % 2 == 0 else n - 1
    near = n - 1 - far
    lead = min(1, far)
    lax.fori_loop(0, lead, beta_step, 0)
    pl.semaphore_wait(barrier, n - 1 + nchol - 1)
    for step in range(lead):
        give(0, step).start()
    lax.fori_loop(lead, far, beta_send, 0)
    lax.fori_loop(far, n - 1, beta_both, 0)
    for r in range(1, nvec):
        def start_both(step, carry, r=r):
            give(r - 1, far + step).start()
            if r == nvec - 1:
                give(r, far + step).start()
            give(r, step).start()
            return carry

        def start_far(step, carry, r=r):
            give(r, step).start()
            return carry

        if r > 1:
            lax.fori_loop(0, near, start_both, 0)
        lax.fori_loop(near, far, start_far, 0)
    load_alpha.start()

    mine = beta_block(n - 1, me)
    for r in range(nvec):
        recv[r][me] = mine[r]
    load_alpha.wait()

    def alpha_block(r, i):
        left = jnp.concatenate([aval[i, m] for m in range(nnz)], axis=1)
        right = jnp.concatenate([recv[r][acols[m, i]] for m in range(nnz)], axis=0)
        return jnp.dot(left, right, preferred_element_type=jnp.float32)

    def alpha_rows(to, r, first):
        group = max(g for g in (4, 2, 1) if share % g == 0)

        def some(at, carry):
            for b in range(group):
                row = at * group + b
                to[pl.ds(pl.multiple_of(row * blk, blk), blk), :] = alpha_block(r, first + row)
            return carry

        lax.fori_loop(0, share // group, some, 0)

    def exchange(o, r):
        return pltpu.make_async_remote_copy(
            src_ref=tsend.at[o - 1, r],
            dst_ref=trecv.at[o - 1, r],
            send_sem=tsend_sem.at[o - 1, r],
            recv_sem=trecv_sem.at[o - 1, r],
            device_id={"str": me, "chol": (core + o) % nchol},
            device_id_type=MESH,
        )

    def store(r):
        return pltpu.make_async_copy(out.at[r], out_hbm.at[r], out_sem.at[r])

    def finish(r):
        for o in range(1, nchol):
            exchange(o, r).wait_recv()
            out[r] += trecv[o - 1, r]
        store(r).start()

    for r in range(nvec):
        if n > 1:
            landed = recv[r].at[pl.ds(0, n - 1)]
            pltpu.make_async_copy(landed, landed, recv_sem.at[r]).wait()
        for o in range(1, nchol):
            alpha_rows(tsend.at[o - 1, r], r, ((core + o) % nchol) * share)
            exchange(o, r).start()
        alpha_rows(out.at[r], r, core * share)
        finish(r)

    for r in range(nvec):
        if n > 1:
            sent = send.at[r, pl.ds(0, n - 1)]
            pltpu.make_async_copy(sent, sent, send_sem.at[r]).wait()
        for o in range(1, nchol):
            exchange(o, r).wait_send()
        store(r).wait()


def body(n, nchol, amplitudes, alpha_values, alpha_cols, beta_values, beta_cols):
    nvec, rows, width = amplitudes.shape
    _, nblk, nnz, blk, _ = beta_values.shape
    assert rows == blk and width == n * blk and nblk == n
    out_rows = nblk * blk // nchol
    dma = pltpu.SemaphoreType.DMA
    others = max(nchol - 1, 1)
    half = (n, blk, blk)
    smem = pl.BlockSpec(memory_space=pltpu.SMEM)
    hbm = pl.BlockSpec(memory_space=pltpu.HBM)
    return pl.pallas_call(
        functools.partial(kernel, n, nchol, nvec, nblk, nnz, blk),
        out_shape=jax.ShapeDtypeStruct((nvec, out_rows, blk), jnp.float32),
        in_specs=[smem, smem, hbm, hbm, hbm],
        out_specs=hbm,
        scratch_shapes=[
            pltpu.VMEM((nblk, nvec, blk, blk), jnp.bfloat16),
            pltpu.VMEM(alpha_values.shape[1:], jnp.bfloat16),
            pltpu.VMEM(beta_values.shape[1:], jnp.bfloat16),
            pltpu.VMEM((nvec,) + half, jnp.bfloat16),
            pltpu.VMEM((others, nvec, out_rows, blk), jnp.float32),
            pltpu.VMEM((others, nvec, out_rows, blk), jnp.float32),
            pltpu.VMEM((nvec, out_rows, blk), jnp.float32),
            *[pltpu.VMEM(half, jnp.bfloat16) for _ in range(nvec)],
            dma((nblk,)), dma, dma((n,)), dma((nvec,)), dma((nvec,)),
            dma((others, nvec)), dma((others, nvec)), dma((nvec,)),
        ],
        compiler_params=pltpu.CompilerParams(
            collective_id=0, has_side_effects=True, vmem_limit_bytes=51 * 1024 * 1024
        ),
        cost_estimate=pl.CostEstimate(
            flops=8 * nvec * nblk * nnz * blk**3, bytes_accessed=2**24, transcendentals=0
        ),
    )(alpha_cols[0].T, beta_cols[0].T, amplitudes, alpha_values[0], beta_values[0])


def solution(mesh):
    placed = (
        P(None, "str", None),
        P("chol", None, None, None, None),
        P("chol", None, None),
        P("chol", None, None, None, None),
        P("chol", None, None),
    )
    return jax.shard_map(
        functools.partial(body, mesh.shape["str"], mesh.shape["chol"]),
        mesh=mesh, in_specs=placed, out_specs=P(None, "chol", "str"), check_vma=False,
    )
```

```python
import functools

import jax
import jax.numpy as jnp
from jax import lax
from jax.experimental import pallas as pl
from jax.experimental.pallas import tpu as pltpu
from jax.sharding import PartitionSpec as P

MESH = pl.DeviceIdType.MESH


def partner(me, step, count):
    if count % 2:
        return (me + 1 + step) % count
    half = count // 2
    side, place = me // half, me % half
    here = step // half
    other = (side + 1 + here) % 2
    return other * half + (place + step + here) % half


def kernel(
    n, nchol, nvec, nblk, nnz, blk,
    cols_in, amp_hbm, aval_hbm, bval_hbm, out,
    cols, amp, aval, bval, send, tsend, trecv, *rest,
):
    recv = rest[:nvec]
    cols_sem, amp_sem, aval_sem, bval_sem, send_sem, recv_sem, tsend_sem, trecv_sem = rest[nvec:]
    me, core = lax.axis_index("str"), lax.axis_index("chol")
    share = nblk // nchol
    group = max(g for g in (4, 2, 1) if share % g == 0)
    pieces = share // group

    barrier = pltpu.get_barrier_semaphore()

    def greet(step, carry):
        pl.semaphore_signal(
            barrier, inc=1, device_id={"str": (me + 1 + step) % n, "chol": core}, device_id_type=MESH
        )
        return carry

    lax.fori_loop(0, n - 1, greet, 0)
    for o in range(1, nchol):
        pl.semaphore_signal(
            barrier, inc=1, device_id={"str": me, "chol": (core + o) % nchol}, device_id_type=MESH
        )
    load_cols = pltpu.make_async_copy(cols_in, cols, cols_sem)
    load_cols.start()

    def load_amp(c):
        return pltpu.make_async_copy(
            amp_hbm.at[:, :, pl.ds(pl.multiple_of(c * blk, blk), blk)], amp.at[c], amp_sem.at[c]
        )

    def start_amp(c, carry):
        load_amp(c).start()
        return carry

    def wait_amp(c, carry):
        load_amp(c).wait()
        return carry

    lax.fori_loop(0, nblk, start_amp, 0)

    def load_beta(step, j):
        return pltpu.make_async_copy(bval_hbm.at[j], bval.at[j], bval_sem.at[step])

    def start_beta(step, carry):
        load_beta(step, partner(me, step, n)).start()
        return carry

    lax.fori_loop(0, n - 1, start_beta, 0)
    load_beta(n - 1, me).start()
    load_alpha = pltpu.make_async_copy(aval_hbm, aval, aval_sem)

    load_cols.wait()
    lax.fori_loop(0, nblk, wait_amp, 0)
    def beta_block(step, j):
        load_beta(step, j).wait()
        total = None
        for m in range(0, nnz, 2):
            left, right = [], []
            for b in range(m, min(m + 2, nnz)):
                left.append(amp[cols[nnz + b, j]].reshape(nvec * blk, blk))
                right.append(bval[j, b])
            part = lax.dot_general(
                jnp.concatenate(left, axis=1), jnp.concatenate(right, axis=1),
                (((1,), (1,)), ((), ())), preferred_element_type=jnp.float32,
            )
            total = part if total is None else total + part
        return total.astype(jnp.bfloat16).reshape(nvec, blk, blk)

    def give(r, step):
        return pltpu.make_async_remote_copy(
            src_ref=send.at[r, step],
            dst_ref=recv[r].at[me],
            send_sem=send_sem.at[r],
            recv_sem=recv_sem.at[r],
            device_id={"str": partner(me, step, n), "chol": core},
            device_id_type=MESH,
        )

    def beta_step(step, carry):
        half = beta_block(step, partner(me, step, n))
        for r in range(nvec):
            send[r, step] = half[r]
        return carry

    def beta_send(step, carry):
        beta_step(step, carry)
        give(0, step).start()
        return carry

    def beta_both(step, carry):
        beta_step(step, carry)
        give(0, step).start()
        if nvec > 1:
            give(1, step - far).start()
        if nvec == 2:
            give(1, step).start()
        return carry

    far = n // 2 if n % 2 == 0 else n - 1
    near = n - 1 - far
    lead = min(1, far)
    lax.fori_loop(0, lead, beta_step, 0)
    pl.semaphore_wait(barrier, n - 1 + nchol - 1)
    for step in range(lead):
        give(0, step).start()
    lax.fori_loop(lead, far, beta_send, 0)
    lax.fori_loop(far, n - 1, beta_both, 0)
    for r in range(1, nvec):
        def start_both(step, carry, r=r):
            give(r - 1, far + step).start()
            if r == nvec - 1:
                give(r, far + step).start()
            give(r, step).start()
            return carry

        def start_far(step, carry, r=r):
            give(r, step).start()
            return carry

        if r > 1:
            lax.fori_loop(0, near, start_both, 0)
        lax.fori_loop(near, far, start_far, 0)
    load_alpha.start()

    mine = beta_block(n - 1, me)
    for r in range(nvec):
        recv[r][me] = mine[r]
    load_alpha.wait()

    def alpha_block(r, i):
        left = jnp.concatenate([aval[i, m] for m in range(nnz)], axis=1)
        right = jnp.concatenate([recv[r][cols[m, i]] for m in range(nnz)], axis=0)
        return jnp.dot(left, right, preferred_element_type=jnp.float32)

    def alpha_rows(to, r, first, at):
        for b in range(group):
            row = at * group + b
            to[pl.ds(pl.multiple_of(row * blk, blk), blk), :] = alpha_block(r, first + row)

    def exchange(o, r, at):
        rows = pl.ds(pl.multiple_of(at * group * blk, group * blk), group * blk)
        return pltpu.make_async_remote_copy(
            src_ref=tsend.at[o - 1, r, rows, :],
            dst_ref=trecv.at[o - 1, r, rows, :],
            send_sem=tsend_sem.at[o - 1, r, at],
            recv_sem=trecv_sem.at[o - 1, r, at],
            device_id={"str": me, "chol": (core + o) % nchol},
            device_id_type=MESH,
        )

    for r in range(nvec):
        if n > 1:
            landed = recv[r].at[pl.ds(0, n - 1)]
            pltpu.make_async_copy(landed, landed, recv_sem.at[r]).wait()
        for o in range(1, nchol):
            def theirs(at, carry, o=o, r=r):
                alpha_rows(tsend.at[o - 1, r], r, ((core + o) % nchol) * share, at)
                exchange(o, r, at).start()
                return carry

            lax.fori_loop(0, pieces, theirs, 0)

        def ours(at, carry, r=r):
            alpha_rows(out.at[r], r, core * share, at)
            return carry

        lax.fori_loop(0, pieces, ours, 0)
        for o in range(1, nchol):
            for at in range(pieces):
                exchange(o, r, at).wait_recv()
                rows = pl.ds(at * group * blk, group * blk)
                out[r, rows, :] += trecv[o - 1, r, rows, :]

    for r in range(nvec):
        if n > 1:
            sent = send.at[r, pl.ds(0, n - 1)]
            pltpu.make_async_copy(sent, sent, send_sem.at[r]).wait()
        for o in range(1, nchol):
            for at in range(pieces):
                exchange(o, r, at).wait_send()


def body(n, nchol, amplitudes, alpha_values, alpha_cols, beta_values, beta_cols):
    nvec, rows, width = amplitudes.shape
    _, nblk, nnz, blk, _ = beta_values.shape
    assert rows == blk and width == n * blk and nblk == n
    out_rows = nblk * blk // nchol
    cols = jnp.concatenate([alpha_cols[0].T, beta_cols[0].T], axis=0)
    dma = pltpu.SemaphoreType.DMA
    others = max(nchol - 1, 1)
    share = nblk // nchol
    pieces = share // max(g for g in (4, 2, 1) if share % g == 0)
    half = (n, blk, blk)
    hbm = pl.BlockSpec(memory_space=pltpu.HBM)
    return pl.pallas_call(
        functools.partial(kernel, n, nchol, nvec, nblk, nnz, blk),
        out_shape=jax.ShapeDtypeStruct((nvec, out_rows, blk), jnp.float32),
        in_specs=[hbm, hbm, hbm, hbm],
        out_specs=pl.BlockSpec(memory_space=pltpu.VMEM),
        scratch_shapes=[
            pltpu.SMEM(cols.shape, jnp.int32),
            pltpu.VMEM((nblk, nvec, blk, blk), jnp.bfloat16),
            pltpu.VMEM(alpha_values.shape[1:], jnp.bfloat16),
            pltpu.VMEM(beta_values.shape[1:], jnp.bfloat16),
            pltpu.VMEM((nvec,) + half, jnp.bfloat16),
            pltpu.VMEM((others, nvec, out_rows, blk), jnp.float32),
            pltpu.VMEM((others, nvec, out_rows, blk), jnp.float32),
            *[pltpu.VMEM(half, jnp.bfloat16) for _ in range(nvec)],
            dma, dma((nblk,)), dma, dma((n,)), dma((nvec,)), dma((nvec,)),
            dma((others, nvec, pieces)), dma((others, nvec, pieces)),
        ],
        compiler_params=pltpu.CompilerParams(
            collective_id=0, has_side_effects=True, vmem_limit_bytes=51 * 1024 * 1024
        ),
        cost_estimate=pl.CostEstimate(
            flops=8 * nvec * nblk * nnz * blk**3, bytes_accessed=2**24, transcendentals=0
        ),
    )(cols, amplitudes, alpha_values[0], beta_values[0])


def solution(mesh):
    placed = (
        P(None, "str", None),
        P("chol", None, None, None, None),
        P("chol", None, None),
        P("chol", None, None, None, None),
        P("chol", None, None),
    )
    return jax.shard_map(
        functools.partial(body, mesh.shape["str"], mesh.shape["chol"]),
        mesh=mesh, in_specs=placed, out_specs=P(None, "chol", "str"), check_vma=False,
    )
```

```python
import functools

import jax
import jax.numpy as jnp
from jax import lax
from jax.experimental import pallas as pl
from jax.experimental.pallas import tpu as pltpu
from jax.sharding import PartitionSpec as P

MESH = pl.DeviceIdType.MESH


def partner(me, step, count):
    if count % 2:
        return (me + 1 + step) % count
    half = count // 2
    side, place = me // half, me % half
    here = step // half
    other = (side + 1 + here) % 2
    turn = (step + here) % half
    if half & (half - 1):
        return other * half + (place + turn) % half
    flipped, bit = 0, 1
    while bit < half:
        flipped += (place // bit + turn // bit) % 2 * bit
        bit *= 2
    return other * half + flipped


def kernel(
    n, nchol, nvec, nblk, nnz, blk,
    cols_in, amp_hbm, aval_hbm, bval_hbm, out,
    cols, amp, aval, bval, send, tsend, trecv, *rest,
):
    recv = rest[:nvec]
    cols_sem, amp_sem, aval_sem, bval_sem, send_sem, recv_sem, tsend_sem, trecv_sem = rest[nvec:]
    me, core = lax.axis_index("str"), lax.axis_index("chol")
    share = nblk // nchol
    group = max(g for g in (4, 2, 1) if share % g == 0)
    pieces = share // group

    barrier = pltpu.get_barrier_semaphore()

    def greet(step, carry):
        pl.semaphore_signal(
            barrier, inc=1, device_id={"str": (me + 1 + step) % n, "chol": core}, device_id_type=MESH
        )
        return carry

    lax.fori_loop(0, n - 1, greet, 0)
    for o in range(1, nchol):
        pl.semaphore_signal(
            barrier, inc=1, device_id={"str": me, "chol": (core + o) % nchol}, device_id_type=MESH
        )
    load_cols = pltpu.make_async_copy(cols_in, cols, cols_sem)
    load_cols.start()

    def load_amp(c):
        return pltpu.make_async_copy(
            amp_hbm.at[:, :, pl.ds(pl.multiple_of(c * blk, blk), blk)], amp.at[c], amp_sem.at[c]
        )

    def start_amp(c, carry):
        load_amp(c).start()
        return carry

    def wait_amp(c, carry):
        load_amp(c).wait()
        return carry

    lax.fori_loop(0, nblk, start_amp, 0)

    def load_beta(step, j):
        return pltpu.make_async_copy(bval_hbm.at[j], bval.at[j], bval_sem.at[step])

    def start_beta(step, carry):
        load_beta(step, partner(me, step, n)).start()
        return carry

    lax.fori_loop(0, n - 1, start_beta, 0)
    load_beta(n - 1, me).start()
    load_alpha = pltpu.make_async_copy(aval_hbm, aval, aval_sem)

    load_cols.wait()
    lax.fori_loop(0, nblk, wait_amp, 0)
    def beta_block(step, j):
        load_beta(step, j).wait()
        total = None
        for m in range(0, nnz, 2):
            left, right = [], []
            for b in range(m, min(m + 2, nnz)):
                left.append(amp[cols[nnz + b, j]].reshape(nvec * blk, blk))
                right.append(bval[j, b])
            part = lax.dot_general(
                jnp.concatenate(left, axis=1), jnp.concatenate(right, axis=1),
                (((1,), (1,)), ((), ())), preferred_element_type=jnp.float32,
            )
            total = part if total is None else total + part
        return total.astype(jnp.bfloat16).reshape(nvec, blk, blk)

    def give(r, step):
        return pltpu.make_async_remote_copy(
            src_ref=send.at[r, step],
            dst_ref=recv[r].at[me],
            send_sem=send_sem.at[r],
            recv_sem=recv_sem.at[r],
            device_id={"str": partner(me, step, n), "chol": core},
            device_id_type=MESH,
        )

    def beta_step(step, carry):
        half = beta_block(step, partner(me, step, n))
        for r in range(nvec):
            send[r, step] = half[r]
        return carry

    def beta_send(step, carry):
        beta_step(step, carry)
        give(0, step).start()
        return carry

    def beta_both(step, carry):
        beta_step(step, carry)
        give(0, step).start()
        if nvec > 1:
            give(1, step - far).start()
        if nvec == 2:
            give(1, step).start()
        return carry

    far = n // 2 if n % 2 == 0 else n - 1
    near = n - 1 - far
    lead = min(1, far)
    lax.fori_loop(0, lead, beta_step, 0)
    pl.semaphore_wait(barrier, n - 1 + nchol - 1)
    for step in range(lead):
        give(0, step).start()
    lax.fori_loop(lead, far, beta_send, 0)
    lax.fori_loop(far, n - 1, beta_both, 0)
    for r in range(1, nvec):
        def start_both(step, carry, r=r):
            give(r - 1, far + step).start()
            if r == nvec - 1:
                give(r, far + step).start()
            give(r, step).start()
            return carry

        def start_far(step, carry, r=r):
            give(r, step).start()
            return carry

        if r > 1:
            lax.fori_loop(0, near, start_both, 0)
        lax.fori_loop(near, far, start_far, 0)
    load_alpha.start()

    mine = beta_block(n - 1, me)
    for r in range(nvec):
        recv[r][me] = mine[r]
    load_alpha.wait()

    def alpha_block(r, i):
        left = jnp.concatenate([aval[i, m] for m in range(nnz)], axis=1)
        right = jnp.concatenate([recv[r][cols[m, i]] for m in range(nnz)], axis=0)
        return jnp.dot(left, right, preferred_element_type=jnp.float32)

    def alpha_rows(to, r, first, at):
        for b in range(group):
            row = at * group + b
            to[pl.ds(pl.multiple_of(row * blk, blk), blk), :] = alpha_block(r, first + row)

    def exchange(o, r, at):
        rows = pl.ds(pl.multiple_of(at * group * blk, group * blk), group * blk)
        return pltpu.make_async_remote_copy(
            src_ref=tsend.at[o - 1, r, rows, :],
            dst_ref=trecv.at[o - 1, r, rows, :],
            send_sem=tsend_sem.at[o - 1, r, at],
            recv_sem=trecv_sem.at[o - 1, r, at],
            device_id={"str": me, "chol": (core + o) % nchol},
            device_id_type=MESH,
        )

    for r in range(nvec):
        if n > 1:
            landed = recv[r].at[pl.ds(0, n - 1)]
            pltpu.make_async_copy(landed, landed, recv_sem.at[r]).wait()
        for o in range(1, nchol):
            def theirs(at, carry, o=o, r=r):
                alpha_rows(tsend.at[o - 1, r], r, ((core + o) % nchol) * share, at)
                exchange(o, r, at).start()
                return carry

            lax.fori_loop(0, pieces, theirs, 0)

        def ours(at, carry, r=r):
            alpha_rows(out.at[r], r, core * share, at)
            return carry

        lax.fori_loop(0, pieces, ours, 0)
        for o in range(1, nchol):
            for at in range(pieces):
                exchange(o, r, at).wait_recv()
                rows = pl.ds(at * group * blk, group * blk)
                out[r, rows, :] += trecv[o - 1, r, rows, :]

    for r in range(nvec):
        if n > 1:
            sent = send.at[r, pl.ds(0, n - 1)]
            pltpu.make_async_copy(sent, sent, send_sem.at[r]).wait()
        for o in range(1, nchol):
            for at in range(pieces):
                exchange(o, r, at).wait_send()


def body(n, nchol, amplitudes, alpha_values, alpha_cols, beta_values, beta_cols):
    nvec, rows, width = amplitudes.shape
    _, nblk, nnz, blk, _ = beta_values.shape
    assert rows == blk and width == n * blk and nblk == n
    out_rows = nblk * blk // nchol
    cols = jnp.concatenate([alpha_cols[0].T, beta_cols[0].T], axis=0)
    dma = pltpu.SemaphoreType.DMA
    others = max(nchol - 1, 1)
    share = nblk // nchol
    pieces = share // max(g for g in (4, 2, 1) if share % g == 0)
    half = (n, blk, blk)
    hbm = pl.BlockSpec(memory_space=pltpu.HBM)
    return pl.pallas_call(
        functools.partial(kernel, n, nchol, nvec, nblk, nnz, blk),
        out_shape=jax.ShapeDtypeStruct((nvec, out_rows, blk), jnp.float32),
        in_specs=[hbm, hbm, hbm, hbm],
        out_specs=pl.BlockSpec(memory_space=pltpu.VMEM),
        scratch_shapes=[
            pltpu.SMEM(cols.shape, jnp.int32),
            pltpu.VMEM((nblk, nvec, blk, blk), jnp.bfloat16),
            pltpu.VMEM(alpha_values.shape[1:], jnp.bfloat16),
            pltpu.VMEM(beta_values.shape[1:], jnp.bfloat16),
            pltpu.VMEM((nvec,) + half, jnp.bfloat16),
            pltpu.VMEM((others, nvec, out_rows, blk), jnp.float32),
            pltpu.VMEM((others, nvec, out_rows, blk), jnp.float32),
            *[pltpu.VMEM(half, jnp.bfloat16) for _ in range(nvec)],
            dma, dma((nblk,)), dma, dma((n,)), dma((nvec,)), dma((nvec,)),
            dma((others, nvec, pieces)), dma((others, nvec, pieces)),
        ],
        compiler_params=pltpu.CompilerParams(
            collective_id=0, has_side_effects=True, vmem_limit_bytes=51 * 1024 * 1024
        ),
        cost_estimate=pl.CostEstimate(
            flops=8 * nvec * nblk * nnz * blk**3, bytes_accessed=2**24, transcendentals=0
        ),
    )(cols, amplitudes, alpha_values[0], beta_values[0])


def solution(mesh):
    placed = (
        P(None, "str", None),
        P("chol", None, None, None, None),
        P("chol", None, None),
        P("chol", None, None, None, None),
        P("chol", None, None),
    )
    return jax.shard_map(
        functools.partial(body, mesh.shape["str"], mesh.shape["chol"]),
        mesh=mesh, in_specs=placed, out_specs=P(None, "chol", "str"), check_vma=False,
    )
```

```python
import functools

import jax
import jax.numpy as jnp
from jax import lax
from jax.experimental import pallas as pl
from jax.experimental.pallas import tpu as pltpu
from jax.sharding import PartitionSpec as P

MESH = pl.DeviceIdType.MESH


def partner(me, step, count):
    if count % 2:
        return (me + 1 + step) % count
    half = count // 2
    side, place = me // half, me % half
    here = step // half
    other = (side + 1 + here) % 2
    turn = (1 - here) * (half - 1 - step) + here * (step + 1 - half)
    if half & (half - 1):
        return other * half + (place + turn) % half
    flipped, bit = 0, 1
    while bit < half:
        flipped += (place // bit + turn // bit) % 2 * bit
        bit *= 2
    return other * half + flipped


def kernel(
    n, nchol, nvec, nblk, nnz, blk,
    cols_in, amp_hbm, aval_hbm, bval_hbm, out,
    cols, amp, aval, bval, send, tsend, trecv, *rest,
):
    recv = rest[:nvec]
    cols_sem, amp_sem, aval_sem, bval_sem, send_sem, recv_sem, tsend_sem, trecv_sem = rest[nvec:]
    me, core = lax.axis_index("str"), lax.axis_index("chol")
    share = nblk // nchol
    group = max(g for g in (4, 2, 1) if share % g == 0)
    pieces = share // group

    barrier = pltpu.get_barrier_semaphore()

    def greet(step, carry):
        pl.semaphore_signal(
            barrier, inc=1, device_id={"str": (me + 1 + step) % n, "chol": core}, device_id_type=MESH
        )
        return carry

    lax.fori_loop(0, n - 1, greet, 0)
    for o in range(1, nchol):
        pl.semaphore_signal(
            barrier, inc=1, device_id={"str": me, "chol": (core + o) % nchol}, device_id_type=MESH
        )
    load_cols = pltpu.make_async_copy(cols_in, cols, cols_sem)
    load_cols.start()

    def load_amp(c):
        return pltpu.make_async_copy(
            amp_hbm.at[:, :, pl.ds(pl.multiple_of(c * blk, blk), blk)], amp.at[c], amp_sem.at[c]
        )

    def start_amp(c, carry):
        load_amp(c).start()
        return carry

    def wait_amp(c, carry):
        load_amp(c).wait()
        return carry

    lax.fori_loop(0, nblk, start_amp, 0)

    def load_beta(step, j):
        return pltpu.make_async_copy(bval_hbm.at[j], bval.at[j], bval_sem.at[step])

    def start_beta(step, carry):
        load_beta(step, partner(me, step, n)).start()
        return carry

    lax.fori_loop(0, n - 1, start_beta, 0)
    load_beta(n - 1, me).start()
    load_alpha = pltpu.make_async_copy(aval_hbm, aval, aval_sem)

    load_cols.wait()
    lax.fori_loop(0, nblk, wait_amp, 0)
    def beta_block(step, j):
        load_beta(step, j).wait()
        total = None
        for m in range(0, nnz, 2):
            left, right = [], []
            for b in range(m, min(m + 2, nnz)):
                left.append(amp[cols[nnz + b, j]].reshape(nvec * blk, blk))
                right.append(bval[j, b])
            part = lax.dot_general(
                jnp.concatenate(left, axis=1), jnp.concatenate(right, axis=1),
                (((1,), (1,)), ((), ())), preferred_element_type=jnp.float32,
            )
            total = part if total is None else total + part
        return total.astype(jnp.bfloat16).reshape(nvec, blk, blk)

    def give(r, step):
        return pltpu.make_async_remote_copy(
            src_ref=send.at[r, step],
            dst_ref=recv[r].at[me],
            send_sem=send_sem.at[r],
            recv_sem=recv_sem.at[r],
            device_id={"str": partner(me, step, n), "chol": core},
            device_id_type=MESH,
        )

    def beta_step(step, carry):
        half = beta_block(step, partner(me, step, n))
        for r in range(nvec):
            send[r, step] = half[r]
        return carry

    def beta_send(step, carry):
        beta_step(step, carry)
        give(0, step).start()
        return carry

    def beta_both(step, carry):
        beta_step(step, carry)
        give(0, step).start()
        if nvec > 1:
            give(1, step - far).start()
        if nvec == 2:
            give(1, step).start()
        return carry

    far = n // 2 if n % 2 == 0 else n - 1
    near = n - 1 - far
    lead = min(1, far)
    lax.fori_loop(0, lead, beta_step, 0)
    pl.semaphore_wait(barrier, n - 1 + nchol - 1)
    for step in range(lead):
        give(0, step).start()
    lax.fori_loop(lead, far, beta_send, 0)
    lax.fori_loop(far, n - 1, beta_both, 0)
    for r in range(1, nvec):
        def start_both(step, carry, r=r):
            give(r - 1, far + step).start()
            if r == nvec - 1:
                give(r, far + step).start()
            give(r, step).start()
            return carry

        def start_far(step, carry, r=r):
            give(r, step).start()
            return carry

        if r > 1:
            lax.fori_loop(0, near, start_both, 0)
        lax.fori_loop(near, far, start_far, 0)
    load_alpha.start()

    mine = beta_block(n - 1, me)
    for r in range(nvec):
        recv[r][me] = mine[r]
    load_alpha.wait()

    def alpha_block(r, i):
        left = jnp.concatenate([aval[i, m] for m in range(nnz)], axis=1)
        right = jnp.concatenate([recv[r][cols[m, i]] for m in range(nnz)], axis=0)
        return jnp.dot(left, right, preferred_element_type=jnp.float32)

    def alpha_rows(to, r, first, at):
        for b in range(group):
            row = at * group + b
            to[pl.ds(pl.multiple_of(row * blk, blk), blk), :] = alpha_block(r, first + row)

    def exchange(o, r, at):
        rows = pl.ds(pl.multiple_of(at * group * blk, group * blk), group * blk)
        return pltpu.make_async_remote_copy(
            src_ref=tsend.at[o - 1, r, rows, :],
            dst_ref=trecv.at[o - 1, r, rows, :],
            send_sem=tsend_sem.at[o - 1, r, at],
            recv_sem=trecv_sem.at[o - 1, r, at],
            device_id={"str": me, "chol": (core + o) % nchol},
            device_id_type=MESH,
        )

    for r in range(nvec):
        if n > 1:
            landed = recv[r].at[pl.ds(0, n - 1)]
            pltpu.make_async_copy(landed, landed, recv_sem.at[r]).wait()
        for o in range(1, nchol):
            def theirs(at, carry, o=o, r=r):
                alpha_rows(tsend.at[o - 1, r], r, ((core + o) % nchol) * share, at)
                exchange(o, r, at).start()
                return carry

            lax.fori_loop(0, pieces, theirs, 0)

        def ours(at, carry, r=r):
            alpha_rows(out.at[r], r, core * share, at)
            return carry

        lax.fori_loop(0, pieces, ours, 0)
        for o in range(1, nchol):
            for at in range(pieces):
                exchange(o, r, at).wait_recv()
                rows = pl.ds(at * group * blk, group * blk)
                out[r, rows, :] += trecv[o - 1, r, rows, :]

    for r in range(nvec):
        if n > 1:
            sent = send.at[r, pl.ds(0, n - 1)]
            pltpu.make_async_copy(sent, sent, send_sem.at[r]).wait()
        for o in range(1, nchol):
            for at in range(pieces):
                exchange(o, r, at).wait_send()


def body(n, nchol, amplitudes, alpha_values, alpha_cols, beta_values, beta_cols):
    nvec, rows, width = amplitudes.shape
    _, nblk, nnz, blk, _ = beta_values.shape
    assert rows == blk and width == n * blk and nblk == n
    out_rows = nblk * blk // nchol
    cols = jnp.concatenate([alpha_cols[0].T, beta_cols[0].T], axis=0)
    dma = pltpu.SemaphoreType.DMA
    others = max(nchol - 1, 1)
    share = nblk // nchol
    pieces = share // max(g for g in (4, 2, 1) if share % g == 0)
    half = (n, blk, blk)
    hbm = pl.BlockSpec(memory_space=pltpu.HBM)
    return pl.pallas_call(
        functools.partial(kernel, n, nchol, nvec, nblk, nnz, blk),
        out_shape=jax.ShapeDtypeStruct((nvec, out_rows, blk), jnp.float32),
        in_specs=[hbm, hbm, hbm, hbm],
        out_specs=pl.BlockSpec(memory_space=pltpu.VMEM),
        scratch_shapes=[
            pltpu.SMEM(cols.shape, jnp.int32),
            pltpu.VMEM((nblk, nvec, blk, blk), jnp.bfloat16),
            pltpu.VMEM(alpha_values.shape[1:], jnp.bfloat16),
            pltpu.VMEM(beta_values.shape[1:], jnp.bfloat16),
            pltpu.VMEM((nvec,) + half, jnp.bfloat16),
            pltpu.VMEM((others, nvec, out_rows, blk), jnp.float32),
            pltpu.VMEM((others, nvec, out_rows, blk), jnp.float32),
            *[pltpu.VMEM(half, jnp.bfloat16) for _ in range(nvec)],
            dma, dma((nblk,)), dma, dma((n,)), dma((nvec,)), dma((nvec,)),
            dma((others, nvec, pieces)), dma((others, nvec, pieces)),
        ],
        compiler_params=pltpu.CompilerParams(
            collective_id=0, has_side_effects=True, vmem_limit_bytes=51 * 1024 * 1024
        ),
        cost_estimate=pl.CostEstimate(
            flops=8 * nvec * nblk * nnz * blk**3, bytes_accessed=2**24, transcendentals=0
        ),
    )(cols, amplitudes, alpha_values[0], beta_values[0])


def solution(mesh):
    placed = (
        P(None, "str", None),
        P("chol", None, None, None, None),
        P("chol", None, None),
        P("chol", None, None, None, None),
        P("chol", None, None),
    )
    return jax.shard_map(
        functools.partial(body, mesh.shape["str"], mesh.shape["chol"]),
        mesh=mesh, in_specs=placed, out_specs=P(None, "chol", "str"), check_vma=False,
    )
```

```python
import functools

import jax
import jax.numpy as jnp
from jax import lax
from jax.experimental import pallas as pl
from jax.experimental.pallas import tpu as pltpu
from jax.sharding import PartitionSpec as P

MESH = pl.DeviceIdType.MESH


def partner(me, step, count):
    if count % 2:
        return (me + 1 + step) % count
    half = count // 2
    side, place = me // half, me % half
    here = step // half
    other = (side + 1 + here) % 2
    turn = (step + here) % half
    if half & (half - 1):
        return other * half + (place + turn) % half
    flipped, bit = 0, 1
    while bit < half:
        flipped += (place // bit + turn // bit) % 2 * bit
        bit *= 2
    return other * half + flipped


def kernel(
    n, nchol, nvec, nblk, nnz, blk,
    cols_in, amp_hbm, aval_hbm, bval_hbm, out,
    cols, amp, aval, bval, send, tsend, trecv, *rest,
):
    recv = rest[:nvec]
    cols_sem, amp_sem, aval_sem, bval_sem, send_sem, recv_sem, tsend_sem, trecv_sem = rest[nvec:]
    me, core = lax.axis_index("str"), lax.axis_index("chol")
    share = nblk // nchol
    group = max(g for g in (4, 2, 1) if share % g == 0)
    pieces = share // group

    barrier = pltpu.get_barrier_semaphore()

    def greet(step, carry):
        pl.semaphore_signal(
            barrier, inc=1, device_id={"str": (me + 1 + step) % n, "chol": core}, device_id_type=MESH
        )
        return carry

    lax.fori_loop(0, n - 1, greet, 0)
    for o in range(1, nchol):
        pl.semaphore_signal(
            barrier, inc=1, device_id={"str": me, "chol": (core + o) % nchol}, device_id_type=MESH
        )
    load_cols = pltpu.make_async_copy(cols_in, cols, cols_sem)
    load_cols.start()

    def load_amp(c):
        return pltpu.make_async_copy(
            amp_hbm.at[:, :, pl.ds(pl.multiple_of(c * blk, blk), blk)], amp.at[c], amp_sem.at[c]
        )

    def start_amp(c, carry):
        load_amp(c).start()
        return carry

    def wait_amp(c, carry):
        load_amp(c).wait()
        return carry

    lax.fori_loop(0, nblk, start_amp, 0)

    def load_beta(step, j):
        return pltpu.make_async_copy(bval_hbm.at[j], bval.at[j], bval_sem.at[step])

    def start_beta(step, carry):
        load_beta(step, partner(me, step, n)).start()
        return carry

    lax.fori_loop(0, n - 1, start_beta, 0)
    load_beta(n - 1, me).start()
    load_alpha = pltpu.make_async_copy(aval_hbm, aval, aval_sem)

    load_cols.wait()
    lax.fori_loop(0, nblk, wait_amp, 0)
    def beta_block(step, j):
        load_beta(step, j).wait()
        total = None
        for m in range(0, nnz, 2):
            left, right = [], []
            for b in range(m, min(m + 2, nnz)):
                left.append(amp[cols[nnz + b, j]].reshape(nvec * blk, blk))
                right.append(bval[j, b])
            part = lax.dot_general(
                jnp.concatenate(left, axis=1), jnp.concatenate(right, axis=1),
                (((1,), (1,)), ((), ())), preferred_element_type=jnp.float32,
            )
            total = part if total is None else total + part
        return total.astype(jnp.bfloat16).reshape(nvec, blk, blk)

    def give(r, step):
        return pltpu.make_async_remote_copy(
            src_ref=send.at[r, step],
            dst_ref=recv[r].at[me],
            send_sem=send_sem.at[r],
            recv_sem=recv_sem.at[r],
            device_id={"str": partner(me, step, n), "chol": core},
            device_id_type=MESH,
        )

    def beta_step(step, carry):
        half = beta_block(step, partner(me, step, n))
        for r in range(nvec):
            send[r, step] = half[r]
        return carry

    def beta_send(step, carry):
        beta_step(step, carry)
        give(0, step).start()
        return carry

    def beta_both(step, carry):
        beta_step(step, carry)
        give(0, step).start()
        if nvec > 1:
            give(1, step - far).start()
        if nvec == 2:
            give(1, step).start()
        return carry

    far = n // 2 if n % 2 == 0 else n - 1
    near = n - 1 - far
    lead = min(1, far)
    lax.fori_loop(0, lead, beta_step, 0)
    pl.semaphore_wait(barrier, n - 1 + nchol - 1)
    for step in range(lead):
        give(0, step).start()
    lax.fori_loop(lead, far, beta_send, 0)
    lax.fori_loop(far, n - 1, beta_both, 0)
    for r in range(1, nvec):
        def start_both(step, carry, r=r):
            give(r, step).start()
            if r == 2:
                give(1, far + step).start()
            give(r, far + step).start()
            return carry

        def start_far(step, carry, r=r):
            give(r, step).start()
            return carry

        if r > 1:
            lax.fori_loop(0, near, start_both, 0)
        lax.fori_loop(near, far, start_far, 0)
    load_alpha.start()

    mine = beta_block(n - 1, me)
    for r in range(nvec):
        recv[r][me] = mine[r]
    load_alpha.wait()

    def alpha_block(r, i):
        left = jnp.concatenate([aval[i, m] for m in range(nnz)], axis=1)
        right = jnp.concatenate([recv[r][cols[m, i]] for m in range(nnz)], axis=0)
        return jnp.dot(left, right, preferred_element_type=jnp.float32)

    def alpha_rows(to, r, first, at):
        for b in range(group):
            row = at * group + b
            to[pl.ds(pl.multiple_of(row * blk, blk), blk), :] = alpha_block(r, first + row)

    def exchange(o, r, at):
        rows = pl.ds(pl.multiple_of(at * group * blk, group * blk), group * blk)
        return pltpu.make_async_remote_copy(
            src_ref=tsend.at[o - 1, r, rows, :],
            dst_ref=trecv.at[o - 1, r, rows, :],
            send_sem=tsend_sem.at[o - 1, r, at],
            recv_sem=trecv_sem.at[o - 1, r, at],
            device_id={"str": me, "chol": (core + o) % nchol},
            device_id_type=MESH,
        )

    for r in range(nvec):
        if n > 1:
            landed = recv[r].at[pl.ds(0, n - 1)]
            pltpu.make_async_copy(landed, landed, recv_sem.at[r]).wait()
        for o in range(1, nchol):
            def theirs(at, carry, o=o, r=r):
                alpha_rows(tsend.at[o - 1, r], r, ((core + o) % nchol) * share, at)
                exchange(o, r, at).start()
                return carry

            lax.fori_loop(0, pieces, theirs, 0)

        def ours(at, carry, r=r):
            alpha_rows(out.at[r], r, core * share, at)
            return carry

        lax.fori_loop(0, pieces, ours, 0)
        for o in range(1, nchol):
            for at in range(pieces):
                exchange(o, r, at).wait_recv()
                rows = pl.ds(at * group * blk, group * blk)
                out[r, rows, :] += trecv[o - 1, r, rows, :]

    for r in range(nvec):
        if n > 1:
            sent = send.at[r, pl.ds(0, n - 1)]
            pltpu.make_async_copy(sent, sent, send_sem.at[r]).wait()
        for o in range(1, nchol):
            for at in range(pieces):
                exchange(o, r, at).wait_send()


def body(n, nchol, amplitudes, alpha_values, alpha_cols, beta_values, beta_cols):
    nvec, rows, width = amplitudes.shape
    _, nblk, nnz, blk, _ = beta_values.shape
    assert rows == blk and width == n * blk and nblk == n
    out_rows = nblk * blk // nchol
    cols = jnp.concatenate([alpha_cols[0].T, beta_cols[0].T], axis=0)
    dma = pltpu.SemaphoreType.DMA
    others = max(nchol - 1, 1)
    share = nblk // nchol
    pieces = share // max(g for g in (4, 2, 1) if share % g == 0)
    half = (n, blk, blk)
    hbm = pl.BlockSpec(memory_space=pltpu.HBM)
    return pl.pallas_call(
        functools.partial(kernel, n, nchol, nvec, nblk, nnz, blk),
        out_shape=jax.ShapeDtypeStruct((nvec, out_rows, blk), jnp.float32),
        in_specs=[hbm, hbm, hbm, hbm],
        out_specs=pl.BlockSpec(memory_space=pltpu.VMEM),
        scratch_shapes=[
            pltpu.SMEM(cols.shape, jnp.int32),
            pltpu.VMEM((nblk, nvec, blk, blk), jnp.bfloat16),
            pltpu.VMEM(alpha_values.shape[1:], jnp.bfloat16),
            pltpu.VMEM(beta_values.shape[1:], jnp.bfloat16),
            pltpu.VMEM((nvec,) + half, jnp.bfloat16),
            pltpu.VMEM((others, nvec, out_rows, blk), jnp.float32),
            pltpu.VMEM((others, nvec, out_rows, blk), jnp.float32),
            *[pltpu.VMEM(half, jnp.bfloat16) for _ in range(nvec)],
            dma, dma((nblk,)), dma, dma((n,)), dma((nvec,)), dma((nvec,)),
            dma((others, nvec, pieces)), dma((others, nvec, pieces)),
        ],
        compiler_params=pltpu.CompilerParams(
            collective_id=0, has_side_effects=True, vmem_limit_bytes=51 * 1024 * 1024
        ),
        cost_estimate=pl.CostEstimate(
            flops=8 * nvec * nblk * nnz * blk**3, bytes_accessed=2**24, transcendentals=0
        ),
    )(cols, amplitudes, alpha_values[0], beta_values[0])


def solution(mesh):
    placed = (
        P(None, "str", None),
        P("chol", None, None, None, None),
        P("chol", None, None),
        P("chol", None, None, None, None),
        P("chol", None, None),
    )
    return jax.shard_map(
        functools.partial(body, mesh.shape["str"], mesh.shape["chol"]),
        mesh=mesh, in_specs=placed, out_specs=P(None, "chol", "str"), check_vma=False,
    )
```
